256 devices in a mesh: tok: 16 (over y, x_hi, core), lat: 16 (over x_lo, z).
Axes of the slice: x: 4 (x_hi: 2, x_lo: 2; x = x_hi * 2 + x_lo), y: 4, z: 8, core: 2. Of those that a mesh axis runs over, the one named last changes fastest.
Arguments:
- tokens: bfloat16 [1024, 3584], P('tok'), may hold values from -8 to 8
- dec_bias: float32 [3584], replicated, may hold values from -3 to 3
- enc_weight: bfloat16 [3584, 131072], P('tok', 'lat'), may hold values from -0.09375 to 0.09375
- enc_bias: float32 [131072], P('lat'), may hold values from -3 to -1
Outputs:
- gram: bfloat16 [4096, 131072], P('tok', 'lat')
The draws below stay inside these ranges and needn't reach their ends.
All inputs are finite; a program needn't handle non-finite values.
Results may differ from the reference program's by a relative error of at most 0.0045.
Values may be sent and summed in bfloat16 or wider, within the bound.
No kernel may reach another device: no remote copies, remote signals or barrier semaphores. Data moves between devices by JAX's collectives and lax.ppermute only.
A program may use at most 128 MiB of HBM per device.

```python
import math
import jax
import jax.numpy as jnp
from jax import lax

D = 3584
LAT = 131072
PANEL = 4096
TOKENS = 1024
N_LAT = 16


def draw_tokens(key, part):
    key = jax.random.fold_in(key, 11)
    first, second = jax.random.split(key, 2)
    row_scale = jnp.exp(jax.random.uniform(first, (TOKENS, 1), jnp.float32, math.log(1.5), math.log(2.25)))
    values = jax.random.normal(second, (TOKENS, D), jnp.float32) * row_scale
    return jnp.clip(values, -8.0, 8.0).astype(jnp.bfloat16)


def block_levels(own_key, extent, pieces, low, top_value):
    gain, own = 1.0, jax.random.fold_in(own_key, 6)
    for dim, blocks in pieces:
        draws = jnp.exp(jax.random.uniform(jax.random.fold_in(own, dim), (blocks,), jnp.float32, low / len(pieces), top_value / len(pieces)))
        gain = gain * jnp.repeat(draws, extent[dim] // blocks).reshape([-1 if axis == dim else 1 for axis in range(len(extent))])
    return gain


def centred(stream_key, extent, deviation, reach, shards=(), kind=jnp.bfloat16):
    loudness = block_levels(stream_key, extent, shards, -0.22, 0.18) if shards else 1.0
    values = jax.random.normal(stream_key, extent, jnp.float32) * deviation * loudness
    return jnp.minimum(jnp.maximum(values, -reach), reach).astype(kind)


def setup_inputs(seed: int = 0) -> dict:
    seeds = jax.random.split(jax.random.key(seed), 5)
    return {
        "tokens": draw_tokens(jax.random.fold_in(seeds[4], 71), 0),
        "dec_bias": centred(seeds[1], (D,), 0.5, 3.0, (), jnp.float32),
        "enc_weight": centred(seeds[2], (D, LAT), D ** -0.5, 0.09375, ((0, 16), (1, 16))),
        "enc_bias": jnp.clip(-3.0 + 2.0 * jax.random.uniform(seeds[3], (LAT,), jnp.float32) ** block_levels(seeds[3], (LAT,), ((0, 16),), -0.2, 0.2), -3.0, -1.0),
    }


def encode(rows, weight, bias):
    pre = jnp.dot(rows, weight, preferred_element_type=jnp.float32) + bias
    return jnp.maximum(pre, 0.0).astype(jnp.bfloat16)


def reference(tokens, dec_bias, enc_weight, enc_bias):
    centered = (tokens.astype(jnp.float32) - dec_bias).astype(jnp.bfloat16)
    panel = encode(centered, enc_weight[:, :PANEL], enc_bias[:PANEL])
    total = centered.shape[0]
    width = LAT // N_LAT

    def one_block(index):
        start = (index * width).astype(jnp.int32)
        weight = lax.dynamic_slice_in_dim(enc_weight, start, width, 1)
        bias = lax.dynamic_slice_in_dim(enc_bias, start, width, 0)
        activity = encode(centered, weight, bias)
        summed = jnp.dot(panel.T, activity, preferred_element_type=jnp.float32)
        return (summed / total).astype(jnp.bfloat16)

    stacked = lax.map(one_block, jnp.arange(N_LAT, dtype=jnp.int32))
    return stacked.transpose(1, 0, 2).reshape(PANEL, LAT)
```

```python
import jax
import jax.numpy as jnp
from jax import lax
from jax.sharding import Mesh, PartitionSpec as P

AXES = ("y", "xh", "c", "xl", "z")
SIZES = (4, 2, 2, 2, 8)
PLANE = ("y", "xh")
TOK = ("y", "xh", "c")
LATENT = ("xl", "z")
CHIPS, CORES, XLO, DEPTH = 8, 2, 2, 8
SWAP = [(0, 1), (1, 0)]


def exchange(block, axes):
    return lax.all_to_all(block, axes, split_axis=0, concat_axis=0, tiled=True)


def spread(block, axes, count):
    copies = jnp.broadcast_to(block[None], (count,) + block.shape)
    return exchange(copies, axes)


def ring(block, step):
    return lax.ppermute(block, "z", [(i, (i + step) % DEPTH) for i in range(DEPTH)])


def per_device(tokens, dec_bias, enc_weight, enc_bias):
    own_tokens, width = tokens.shape
    rows, slab = enc_weight.shape
    half = slab // 2
    cols = half // CHIPS
    total = own_tokens * CHIPS * CORES
    core = lax.axis_index("c")
    chip = lax.axis_index("y") * 2 + lax.axis_index("xh")
    depth = lax.axis_index("z")

    centered = (tokens.astype(jnp.float32) - dec_bias).astype(jnp.bfloat16)
    by_core = centered.reshape(own_tokens, CHIPS, CORES, rows).transpose(2, 0, 1, 3)
    by_core = by_core.reshape(CORES, own_tokens, CHIPS * rows)
    keep = jnp.where(core == 0, by_core[0], by_core[1])
    give = jnp.where(core == 0, by_core[1], by_core[0])
    got = lax.ppermute(give, "c", SWAP)
    pair = jnp.where(core == 0, jnp.stack([keep, got]), jnp.stack([got, keep]))
    pair = pair.reshape(CORES * own_tokens, CHIPS * rows)
    batch = spread(pair, PLANE, CHIPS).reshape(total, CHIPS * rows)

    grouped = enc_weight.reshape(rows, 2, CHIPS, cols)
    acts = []
    for h in range(2):
        weight = exchange(grouped[:, h].transpose(1, 0, 2), PLANE)
        part = jnp.dot(batch, weight.reshape(CHIPS * rows, cols), preferred_element_type=jnp.float32)
        other = lax.ppermute(part, "c", SWAP)
        bias = lax.dynamic_slice_in_dim(enc_bias, h * half + chip * cols, cols)
        acts.append(jnp.maximum(part + other + bias, 0.0).astype(jnp.bfloat16))
    activity = jnp.concatenate(acts, axis=1)

    share = cols // CORES
    piece = share // (XLO * DEPTH)
    mine = jnp.where(core == 0, acts[0][:, :share], acts[0][:, share:]).T
    mine = mine.reshape(DEPTH, XLO, piece, total).transpose(1, 0, 2, 3)
    mine = mine.reshape(XLO * DEPTH, piece, total)
    held = exchange(mine, LATENT)[0]
    block = spread(held, ("y", "xh", "xl"), CHIPS * XLO)
    block = block.reshape(CHIPS, XLO * piece, total)

    strip = XLO * piece

    def gram(blocks):
        n = blocks.shape[0]
        out = lax.dot_general(
            blocks.reshape(-1, total), activity, (((1,), (0,)), ((), ())),
            preferred_element_type=jnp.float32,
        )
        out = (out / total).astype(jnp.bfloat16)
        return out.reshape(n, CHIPS, strip, 2 * cols)

    def send(blocks):
        n = len(blocks)
        out = gram(jnp.stack(blocks)).transpose(1, 0, 2, 3)
        out = exchange(out, PLANE)
        out = out.reshape(CHIPS, n, strip, 2, cols).transpose(1, 2, 3, 0, 4)
        return out.reshape(n, strip, slab)

    result = jnp.zeros((share, slab), jnp.bfloat16)

    def place(result, strips, offsets):
        for i, off in enumerate(offsets):
            start = lax.rem(depth + off + DEPTH, DEPTH) * strip
            result = lax.dynamic_update_slice_in_dim(result, strips[i], start, axis=0)
        return result

    up = down = block
    result = place(result, send([block]), [0])
    for step in range(1, DEPTH // 2):
        up, down = ring(up, 1), ring(down, -1)
        result = place(result, send([up, down]), [-step, step])
    cut = CHIPS // 2
    last = jnp.concatenate([ring(up[:cut], 1), ring(down[cut:], -1)])
    return place(result, send([last]), [DEPTH // 2])


def solution(mesh):
    fine = Mesh(mesh.devices.reshape(SIZES), AXES)
    return jax.shard_map(
        per_device,
        mesh=fine,
        in_specs=(P(TOK, None), P(), P(TOK, LATENT), P(LATENT)),
        out_specs=P(TOK, LATENT),
        check_vma=False,
    )
```

```python
import jax
import jax.numpy as jnp
from jax import lax
from jax.experimental import pallas as pl
from jax.experimental.pallas import tpu as pltpu
from jax.sharding import Mesh, PartitionSpec as P

AXES = ("y", "xh", "c", "xl", "z")
SIZES = (4, 2, 2, 2, 8)
PLANE = ("y", "xh", "xl")
TOK = ("y", "xh", "c")
LATENT = ("xl", "z")
CHIPS, CORES, XLO, DEPTH = 8, 2, 2, 8
SWAP = [(0, 1), (1, 0)]
UP = [(i, (i + 1) % DEPTH) for i in range(DEPTH)]
DOWN = [(i, (i - 1) % DEPTH) for i in range(DEPTH)]


def exchange(block):
    return lax.all_to_all(block, PLANE, split_axis=0, concat_axis=0, tiled=True)


def spread(block):
    return exchange(jnp.broadcast_to(block[None], (CHIPS * XLO,) + block.shape))


def other_half(block):
    cut = block.shape[0] // 2
    return lax.ppermute(block[:cut], "z", UP), lax.ppermute(block[cut:], "z", DOWN)


def place(received, parity, strip, slab, base=None):
    lane = slab // (2 * CHIPS * CORES * XLO)

    def body(par_ref, in_ref, *rest):
        out_ref = rest[-1]
        for xl in range(XLO):
            for c in range(CORES):
                at = (c * XLO + xl) * lane
                out_ref[:, 0, :, at : at + lane] = in_ref[0, xl, :, :, c * lane : (c + 1) * lane]

    width = CORES * XLO * lane
    data = received.reshape(CHIPS, XLO, XLO, strip, 2 * CORES * lane)
    in_specs = [
        pl.BlockSpec((1, XLO, XLO, strip, CORES * lane), lambda h, t, par: (t, 0, 0, 0, h))
    ]
    args = [parity, data]
    if base is not None:
        in_specs.append(pl.BlockSpec(memory_space=pl.ANY))
        args.append(base)
    return pl.pallas_call(
        body,
        out_shape=jax.ShapeDtypeStruct((XLO, 2, strip, slab), jnp.bfloat16),
        grid_spec=pltpu.PrefetchScalarGridSpec(
            num_scalar_prefetch=1,
            grid=(2, CHIPS),
            in_specs=in_specs,
            out_specs=pl.BlockSpec(
                (XLO, 1, strip, width), lambda h, t, par: (0, par[0], 0, h * CHIPS + t)
            ),
        ),
        input_output_aliases={} if base is None else {2: 0},
        cost_estimate=pl.CostEstimate(
            flops=0, bytes_accessed=2 * 2 * XLO * strip * slab, transcendentals=0
        ),
    )(*args)


def per_device(tokens, dec_bias, enc_weight, enc_bias):
    own, width = tokens.shape
    rows, slab = enc_weight.shape
    lane = slab // (2 * CHIPS * CORES * XLO)
    total = own * CHIPS * CORES
    core = lax.axis_index("c")
    xlo = lax.axis_index("xl")
    chip = lax.axis_index("y") * 2 + lax.axis_index("xh")
    z = lax.axis_index("z")
    odd = lax.rem(z, 2)

    centered = (tokens.astype(jnp.float32) - dec_bias).astype(jnp.bfloat16)
    halves = centered.reshape(own, CHIPS, CORES, rows).transpose(2, 0, 1, 3)
    halves = halves.reshape(CORES, own, CHIPS * rows)
    keep = jnp.where(core == 0, halves[0], halves[1])
    give = jnp.where(core == 0, halves[1], halves[0])
    got = lax.ppermute(give, "c", SWAP)
    mine = jnp.where(core == xlo, keep, got)
    part = own // 2
    mine = jnp.where(odd == 0, mine[:part], mine[part:])
    near = spread(mine).reshape(total // 2, CHIPS * rows)
    far = jnp.concatenate(other_half(near))
    batch = jnp.where(odd == 0, jnp.concatenate([near, far]), jnp.concatenate([far, near]))

    biases = enc_bias.reshape(2, CHIPS, CORES, XLO, lane)
    biases = lax.dynamic_index_in_dim(biases, chip, 1, keepdims=False)
    bias_keep = lax.dynamic_index_in_dim(biases, xlo, 2, keepdims=False)
    bias_give = lax.dynamic_index_in_dim(biases, 1 - xlo, 2, keepdims=False)
    bias_got = lax.ppermute(bias_give, "xl", SWAP)
    bias = jnp.where(xlo == 0, jnp.stack([bias_keep, bias_got]), jnp.stack([bias_got, bias_keep]))

    grouped = enc_weight.reshape(rows, 2, CHIPS, CORES, XLO, lane).transpose(1, 2, 4, 0, 3, 5)
    grouped = grouped.reshape(2, CHIPS * XLO, rows, CORES * lane)

    def encode(h):
        weight = exchange(grouped[h]).reshape(CHIPS, XLO, rows, CORES * lane)
        weight = weight.transpose(0, 2, 1, 3).reshape(CHIPS * rows, XLO * CORES * lane)
        pre = jnp.dot(batch, weight, preferred_element_type=jnp.float32)
        other = lax.ppermute(pre, "c", SWAP)
        pre = pre + other + bias[:, h].reshape(XLO * CORES * lane)
        return jnp.maximum(pre, 0.0).astype(jnp.bfloat16)

    first = encode(0)

    panel = jnp.where(core == 0, first[:, :lane], first[:, lane : 2 * lane]).T
    strip = lane // 2
    held = jnp.where(z == 0, panel[:strip], jnp.zeros_like(panel[:strip]))
    for d in range(1, DEPTH):
        piece = panel[(d % 2) * strip : (d % 2 + 1) * strip]
        held = held + lax.ppermute(piece, "z", [(0, d)])

    second = encode(1)
    block = spread(held)
    activity = jnp.concatenate([first, second], axis=1).reshape(total, 2, XLO, CORES * lane)
    activity = activity.transpose(0, 2, 1, 3).reshape(total, XLO * 2 * CORES * lane)

    def gram(rows_of):
        out = lax.dot_general(
            rows_of.reshape(-1, total), activity, (((1,), (0,)), ((), ())),
            preferred_element_type=jnp.float32,
        )
        out = (out / total).astype(jnp.bfloat16)
        out = out.reshape(CHIPS, XLO * strip, XLO, 2 * CORES * lane).transpose(0, 2, 1, 3)
        return exchange(out.reshape(CHIPS * XLO, XLO * strip, 2 * CORES * lane))

    side = jnp.reshape(odd, (1,))
    rest = jnp.concatenate(other_half(block))
    result = place(gram(block), side, strip, slab)
    result = place(gram(rest), 1 - side, strip, slab, result)
    return result.reshape(XLO * 2 * strip, slab)


def solution(mesh):
    fine = Mesh(mesh.devices.reshape(SIZES), AXES)
    return jax.shard_map(
        per_device,
        mesh=fine,
        in_specs=(P(TOK, None), P(), P(TOK, LATENT), P(LATENT)),
        out_specs=P(TOK, LATENT),
        check_vma=False,
    )
```

```python
import jax
import jax.numpy as jnp
from jax import lax
from jax.experimental import pallas as pl
from jax.experimental.pallas import tpu as pltpu
from jax.sharding import Mesh, PartitionSpec as P

AXES = ("y", "xh", "c", "xl", "z")
SIZES = (4, 2, 2, 2, 8)
PLANE = ("y", "xh", "xl")
ROW = ("xh", "c", "xl")
TOK = ("y", "xh", "c")
LATENT = ("xl", "z")
YS, CHIPS, CORES, XLO, DEPTH = 4, 8, 2, 2, 8
PEERS = CHIPS * XLO
MATES = 8
SWAP = [(0, 1), (1, 0)]
VMEM = 60 * 1024 * 1024
ORDER = ((0, 0), (-1, 0), (1, 0), (-2, 0), (2, 0), (-3, 0), (3, 0), (4, 0), (4, 1))


def shift(axis, step):
    size = SIZES[AXES.index(axis)]
    return [(i, (i + step) % size) for i in range(size)]


def params(**kw):
    return pltpu.CompilerParams(vmem_limit_bytes=VMEM, **kw)


def cost(flops, moved):
    return pl.CostEstimate(flops=flops, bytes_accessed=moved, transcendentals=0)


def exchange(block, axes):
    return lax.all_to_all(block, axes, split_axis=0, concat_axis=0, tiled=True)


def spread(block, axes, count):
    return exchange(jnp.broadcast_to(block[None], (count,) + block.shape), axes)


def regroup(weight, lane):
    rows = weight.shape[0]

    def body(in_ref, out_ref):
        for xl in range(XLO):
            for c in range(CORES):
                at = (c * XLO + xl) * lane
                out_ref[xl, :, c * lane : (c + 1) * lane] = in_ref[:, at : at + lane]

    return pl.pallas_call(
        body,
        out_shape=jax.ShapeDtypeStruct((PEERS, rows, 2 * CORES * lane), weight.dtype),
        grid=(2, CHIPS),
        in_specs=[pl.BlockSpec((rows, CORES * XLO * lane), lambda h, t: (0, h * CHIPS + t))],
        out_specs=pl.BlockSpec((XLO, rows, CORES * lane), lambda h, t: (t, 0, h)),
        cost_estimate=cost(0, 4 * PEERS * rows * 2 * CORES * lane),
        compiler_params=params(),
    )(weight)


def encode(place_ids, pieces, weight, lane):
    depth = pieces[0].shape[1]
    _, rows, cols = weight.shape
    strip = pieces[0].shape[0]
    total, wide = DEPTH * strip, XLO * cols
    chunk = 2 * strip
    count = len(pieces)

    def body(ids_ref, *refs):
        weight_ref, keep_ref, give_ref, batch, grid, sems = refs[count:]
        z, core = ids_ref[0], ids_ref[1]
        copies = [
            pltpu.make_async_copy(
                weight_ref.at[p],
                grid.at[pl.ds((p // XLO) * rows, rows), pl.ds((p % XLO) * cols, cols)],
                sems.at[p],
            )
            for p in range(PEERS)
        ]
        for i, (ref, (step, cut)) in enumerate(zip(refs[:count], ORDER)):
            start = lax.rem(z + step + DEPTH, DEPTH) * strip + cut * (strip // 2)
            at = pl.ds(pl.multiple_of(start, strip // 2), ref.shape[0])
            copies.append(pltpu.make_async_copy(ref, batch.at[at], sems.at[PEERS + i]))
        for copy in copies:
            copy.start()
        for copy in copies:
            copy.wait()

        @pl.loop(0, total // chunk)
        def _(i):
            at = pl.ds(pl.multiple_of(i * chunk, chunk), chunk)
            for xl in range(XLO):
                out = jnp.dot(
                    batch[at], grid[:, xl * cols : (xl + 1) * cols],
                    preferred_element_type=jnp.float32,
                )
                for h in range(2):
                    a = out[:, 2 * h * lane : (2 * h + 1) * lane]
                    b = out[:, (2 * h + 1) * lane : (2 * h + 2) * lane]
                    to = pl.ds((xl * 2 + h) * lane, lane)
                    keep_ref[at, to] = jnp.where(core == 0, a, b)
                    give_ref[at, to] = jnp.where(core == 0, b, a).astype(jnp.bfloat16)

    mine = wide // CORES
    return pl.pallas_call(
        body,
        out_shape=(
            jax.ShapeDtypeStruct((total, mine), jnp.float32),
            jax.ShapeDtypeStruct((total, mine), jnp.bfloat16),
        ),
        in_specs=[pl.BlockSpec(memory_space=pltpu.SMEM)]
        + [pl.BlockSpec(memory_space=pl.ANY)] * (count + 1),
        out_specs=(pl.BlockSpec(memory_space=pltpu.VMEM), pl.BlockSpec(memory_space=pltpu.VMEM)),
        scratch_shapes=[
            pltpu.VMEM((total, depth), jnp.bfloat16),
            pltpu.VMEM((CHIPS * rows, wide), jnp.bfloat16),
            pltpu.SemaphoreType.DMA((PEERS + count,)),
        ],
        cost_estimate=cost(2 * total * depth * wide, 2 * depth * (total + wide) + 6 * total * mine),
        compiler_params=params(),
    )(place_ids, *pieces, weight)


def gram(panel, own, below, above, far_low, far_high):
    _, strip, total = panel.shape
    wide = own.shape[1]
    cols = wide // XLO
    height = XLO * strip
    cut = total // 2

    def body(panel_ref, own_ref, below_ref, above_ref, low_ref, high_ref, out_ref):
        rows = panel_ref[...].reshape(height, total)
        for r in range(YS):
            if r < 3:
                ref = (own_ref, below_ref, above_ref)[r]
                out = jnp.dot(rows, ref[...], preferred_element_type=jnp.float32)
            else:
                out = jnp.dot(rows[:, :cut], low_ref[...], preferred_element_type=jnp.float32)
                out += jnp.dot(rows[:, cut:], high_ref[...], preferred_element_type=jnp.float32)
            out = (out * (1.0 / total)).astype(jnp.bfloat16)
            for xl in range(XLO):
                out_ref[xl, :, r * cols : (r + 1) * cols] = out[:, xl * cols : (xl + 1) * cols]

    def whole(a):
        return pl.BlockSpec(a.shape, lambda t: (0, 0))

    acts = (own, below, above, far_low, far_high)
    return pl.pallas_call(
        body,
        out_shape=jax.ShapeDtypeStruct((MATES, height, YS * cols), jnp.bfloat16),
        grid=(MATES // XLO,),
        in_specs=[pl.BlockSpec((XLO, strip, total), lambda t: (t, 0, 0))] + [whole(a) for a in acts],
        out_specs=pl.BlockSpec((XLO, height, YS * cols), lambda t: (t, 0, 0)),
        cost_estimate=cost(
            2 * (MATES // XLO) * height * total * YS * wide,
            2 * (MATES * strip * total + YS * total * wide + MATES * height * YS * cols),
        ),
        compiler_params=params(),
    )(panel, *acts)


def place(ys, received, lane):
    _, height, wide = received.shape
    slab = MATES * wide

    def body(ys_ref, in_ref, out_ref):
        for s in range(MATES):
            out_ref[:, s * lane : (s + 1) * lane] = in_ref[s]

    return pl.pallas_call(
        body,
        out_shape=jax.ShapeDtypeStruct((height, slab), jnp.bfloat16),
        grid_spec=pltpu.PrefetchScalarGridSpec(
            num_scalar_prefetch=1,
            grid=(YS, 2),
            in_specs=[pl.BlockSpec((MATES, height, lane), lambda r, h, ys: (0, 0, 2 * r + h))],
            out_specs=pl.BlockSpec((height, MATES * lane), lambda r, h, ys: (0, h * YS + ys[r])),
        ),
        cost_estimate=cost(0, 4 * height * slab),
        compiler_params=params(),
    )(ys, received)


def per_device(tokens, dec_bias, enc_weight, enc_bias):
    own, width = tokens.shape
    rows, slab = enc_weight.shape
    lane = slab // (2 * CHIPS * CORES * XLO)
    total = own * CHIPS * CORES
    core = lax.axis_index("c")
    xlo = lax.axis_index("xl")
    y = lax.axis_index("y")
    chip = y * 2 + lax.axis_index("xh")
    z = lax.axis_index("z")
    ids = jnp.stack([z, core]).astype(jnp.int32)
    ys = lax.rem(jnp.stack([y, y + 3, y + 1, y + 2]), YS).astype(jnp.int32)

    centered = (tokens.astype(jnp.float32) - dec_bias).astype(jnp.bfloat16)
    halves = centered.reshape(own, CHIPS, CORES, rows).transpose(2, 0, 1, 3)
    halves = halves.reshape(CORES, own, CHIPS * rows)
    keep = jnp.where(core == 0, halves[0], halves[1])
    give = jnp.where(core == 0, halves[1], halves[0])
    got = lax.ppermute(give, "c", SWAP)
    mine = jnp.where(core == xlo, keep, got)
    part = own // DEPTH
    mine = lax.dynamic_slice_in_dim(mine, z * part, part, 0)
    near = spread(mine, PLANE, PEERS).reshape(total // DEPTH, CHIPS * rows)
    pieces = [near]
    low = high = near
    for _ in range(DEPTH // 2 - 1):
        low = lax.ppermute(low, "z", shift("z", 1))
        high = lax.ppermute(high, "z", shift("z", -1))
        pieces += [low, high]
    cut = near.shape[0] // 2
    pieces.append(lax.ppermute(low[:cut], "z", shift("z", 1)))
    pieces.append(lax.ppermute(high[cut:], "z", shift("z", -1)))

    biases = enc_bias.reshape(2, CHIPS, CORES, XLO, lane)
    biases = lax.dynamic_index_in_dim(biases, chip, 1, keepdims=False)
    biases = lax.dynamic_index_in_dim(biases, core, 1, keepdims=False)
    bias_keep = lax.dynamic_index_in_dim(biases, xlo, 1, keepdims=False)
    bias_give = lax.dynamic_index_in_dim(biases, 1 - xlo, 1, keepdims=False)
    bias_got = lax.ppermute(bias_give, "xl", SWAP)
    bias = jnp.where(xlo == 0, jnp.stack([bias_keep, bias_got]), jnp.stack([bias_got, bias_keep]))

    weight = exchange(regroup(enc_weight, lane), PLANE)
    sums, sent = encode(ids, pieces, weight, lane)
    other = lax.ppermute(sent, "c", SWAP).astype(jnp.float32)
    activity = jnp.maximum(sums + other + bias.reshape(-1), 0.0).astype(jnp.bfloat16)

    panel = activity[:, :lane].T
    held = panel
    span = DEPTH // 2
    while span:
        moved = lax.ppermute(held, "z", [(i, i + span) for i in range(0, DEPTH, 2 * span)])
        held = jnp.where(lax.rem(z, 2 * span) == span, moved, held)
        span //= 2

    cut = total // 2
    below = lax.ppermute(activity, "y", shift("y", 1))
    above = lax.ppermute(activity, "y", shift("y", -1))
    held, below, above = lax.optimization_barrier((held, below, above))
    panel = spread(held, ROW, MATES)
    far_low = lax.ppermute(above[:cut], "y", shift("y", -1))
    far_high = lax.ppermute(below[cut:], "y", shift("y", 1))

    result = exchange(gram(panel, activity, below, above, far_low, far_high), ROW)
    return place(ys, result, lane)


def solution(mesh):
    fine = Mesh(mesh.devices.reshape(SIZES), AXES)
    return jax.shard_map(
        per_device,
        mesh=fine,
        in_specs=(P(TOK, None), P(), P(TOK, LATENT), P(LATENT)),
        out_specs=P(TOK, LATENT),
        check_vma=False,
    )
```

```python
import jax
import jax.numpy as jnp
from jax import lax
from jax.experimental import pallas as pl
from jax.experimental.pallas import tpu as pltpu
from jax.sharding import Mesh, PartitionSpec as P

AXES = ("y", "xh", "c", "xl", "z")
SIZES = (4, 2, 2, 2, 8)
PLANE = ("y", "xh", "xl")
ROW = ("xh", "c", "xl")
LINE = ("xh", "xl")
TOK = ("y", "xh", "c")
LATENT = ("xl", "z")
YS, CHIPS, CORES, XLO, DEPTH = 4, 8, 2, 2, 8
PEERS = CHIPS * XLO
MATES = 8
SWAP = [(0, 1), (1, 0)]
VMEM = 60 * 1024 * 1024
ORDER = ((0, 0), (-1, 0), (1, 0), (-2, 0), (2, 0), (-3, 0), (3, 0), (4, 0), (4, 1))


def shift(axis, step):
    size = SIZES[AXES.index(axis)]
    return [(i, (i + step) % size) for i in range(size)]


def params(limit=VMEM):
    return pltpu.CompilerParams(vmem_limit_bytes=limit)


def cost(flops, moved):
    return pl.CostEstimate(flops=flops, bytes_accessed=moved, transcendentals=0)


def exchange(block, axes):
    return lax.all_to_all(block, axes, split_axis=0, concat_axis=0, tiled=True)


def spread(block, axes, count):
    return exchange(jnp.broadcast_to(block[None], (count,) + block.shape), axes)


def regroup(weight, lane):
    rows = weight.shape[0]
    group = 4

    def body(in_ref, out_ref):
        for t in range(group):
            for xl in range(XLO):
                for c in range(CORES):
                    at = ((t * CORES + c) * XLO + xl) * lane
                    to = slice(c * lane, (c + 1) * lane)
                    out_ref[t * XLO + xl, :, to] = in_ref[:, at : at + lane]

    wide = group * CORES * XLO * lane
    steps = CHIPS // group
    return pl.pallas_call(
        body,
        out_shape=jax.ShapeDtypeStruct((PEERS, rows, 2 * CORES * lane), weight.dtype),
        grid=(2, steps),
        in_specs=[pl.BlockSpec((rows, wide), lambda h, t: (0, h * steps + t))],
        out_specs=pl.BlockSpec((group * XLO, rows, CORES * lane), lambda h, t: (t, 0, h)),
        cost_estimate=cost(0, 4 * PEERS * rows * 2 * CORES * lane),
        compiler_params=params(),
    )(weight)


def collect(z, pieces):
    strip, depth = pieces[0].shape
    count = len(pieces)

    def body(z_ref, *refs):
        out_ref, sems = refs[-2:]
        copies = []
        for i, (step, cut) in enumerate(ORDER):
            start = lax.rem(z_ref[0] + step + DEPTH, DEPTH) * strip + cut * (strip // 2)
            at = pl.ds(pl.multiple_of(start, strip // 2), refs[i].shape[0])
            copies.append(pltpu.make_async_copy(refs[i], out_ref.at[at], sems.at[i]))
        for copy in copies:
            copy.start()
        for copy in copies:
            copy.wait()

    return pl.pallas_call(
        body,
        out_shape=jax.ShapeDtypeStruct((DEPTH * strip, depth), pieces[0].dtype),
        in_specs=[pl.BlockSpec(memory_space=pltpu.SMEM)]
        + [pl.BlockSpec(memory_space=pl.ANY)] * count,
        out_specs=pl.BlockSpec(memory_space=pl.ANY),
        scratch_shapes=[pltpu.SemaphoreType.DMA((count,))],
        cost_estimate=cost(0, 4 * DEPTH * strip * depth),
        compiler_params=params(16 * 1024 * 1024),
    )(z, *pieces)


def encode(core, batch, weight, lane):
    total, depth = batch.shape
    _, rows, cols = weight.shape
    wide = XLO * cols
    chunk = total // 4

    def body(core_ref, batch_ref, weight_ref, keep_ref, give_ref, grid, sems):
        slabs = [
            [
                pltpu.make_async_copy(
                    weight_ref.at[t * XLO + xl],
                    grid.at[xl, pl.ds(t * rows, rows)],
                    sems.at[t * XLO + xl],
                )
                for t in range(CHIPS)
            ]
            for xl in range(XLO)
        ]
        xl, i = pl.program_id(0), pl.program_id(1)

        @pl.when((xl == 0) & (i == 0))
        def _():
            for copy in slabs[0] + slabs[1]:
                copy.start()
            for copy in slabs[0]:
                copy.wait()

        @pl.when((xl == 1) & (i == 0))
        def _():
            for copy in slabs[1]:
                copy.wait()

        at = pl.ds(pl.multiple_of(i * chunk, chunk), chunk)
        out = jnp.dot(batch_ref[at], grid[xl], preferred_element_type=jnp.float32)
        for h in range(2):
            a = out[:, 2 * h * lane : (2 * h + 1) * lane]
            b = out[:, (2 * h + 1) * lane : (2 * h + 2) * lane]
            keep_ref[:, h * lane : (h + 1) * lane] = jnp.where(core_ref[0] == 0, a, b)
            give_ref[:, h * lane : (h + 1) * lane] = jnp.where(core_ref[0] == 0, b, a)

    mine = wide // CORES
    block = pl.BlockSpec((chunk, 2 * lane), lambda xl, i: (i, xl))
    return pl.pallas_call(
        body,
        out_shape=(
            jax.ShapeDtypeStruct((total, mine), jnp.float32),
            jax.ShapeDtypeStruct((total, mine), jnp.float32),
        ),
        grid=(XLO, total // chunk),
        in_specs=[
            pl.BlockSpec(memory_space=pltpu.SMEM),
            pl.BlockSpec(memory_space=pltpu.VMEM),
            pl.BlockSpec(memory_space=pl.ANY),
        ],
        out_specs=(block, block),
        scratch_shapes=[
            pltpu.VMEM((XLO, CHIPS * rows, cols), jnp.bfloat16),
            pltpu.SemaphoreType.DMA((PEERS,)),
        ],
        cost_estimate=cost(2 * total * depth * wide, 2 * depth * (total + wide) + 8 * total * mine),
        compiler_params=params(58 * 1024 * 1024),
    )(core, batch, weight)


def finish(sums, other, bias):
    total, wide = sums.shape
    lane = wide // (2 * XLO)
    half = total // 2
    chunk = half // 2

    def body(low_sums, high_sums, low_other, high_other, bias_ref, low_ref, high_ref, *turned):
        refs = ((low_sums, low_other, low_ref), (high_sums, high_other, high_ref))
        for (sums_ref, other_ref, act_ref), turned_ref in zip(refs, turned):
            act = jnp.maximum(sums_ref[...] + other_ref[...] + bias_ref[...], 0.0)
            act_ref[...] = act.astype(jnp.bfloat16)
            turned_ref[...] = act[:, :lane].T.astype(jnp.bfloat16)

    steps = half // chunk
    low = pl.BlockSpec((chunk, wide), lambda i: (i, 0))
    high = pl.BlockSpec((chunk, wide), lambda i: (i + steps, 0))
    turned = pl.BlockSpec((lane, chunk), lambda i: (0, i))
    return pl.pallas_call(
        body,
        out_shape=(jax.ShapeDtypeStruct((half, wide), jnp.bfloat16),) * 2
        + (jax.ShapeDtypeStruct((lane, half), jnp.bfloat16),) * 2,
        grid=(steps,),
        in_specs=[low, high, low, high, pl.BlockSpec((1, wide), lambda i: (0, 0))],
        out_specs=(low, low, turned, turned),
        cost_estimate=cost(0, 10 * total * wide),
        compiler_params=params(8 * 1024 * 1024),
    )(sums, sums, other, other, bias.reshape(1, wide))


def assemble(here, parts, size):
    strip, total = parts[0].shape
    order = (0, -1, 1, 2)

    def body(here_ref, *refs):
        out_ref, sems = refs[-2:]
        copies = []
        for i, step in enumerate(order):
            slot = lax.rem(here_ref[0] + step + size, size)
            copies.append(pltpu.make_async_copy(refs[i], out_ref.at[slot], sems.at[i]))
        for copy in copies:
            copy.start()
        for copy in copies:
            copy.wait()

    return pl.pallas_call(
        body,
        out_shape=jax.ShapeDtypeStruct((size, strip, total), parts[0].dtype),
        in_specs=[pl.BlockSpec(memory_space=pltpu.SMEM)]
        + [pl.BlockSpec(memory_space=pl.ANY)] * len(order),
        out_specs=pl.BlockSpec(memory_space=pl.ANY),
        scratch_shapes=[pltpu.SemaphoreType.DMA((len(order),))],
        cost_estimate=cost(0, 4 * size * strip * total),
        compiler_params=params(16 * 1024 * 1024),
    )(here, *parts)


def gram(core, mine, theirs, acts):
    _, strip, total = mine.shape
    wide = acts[0].shape[1]
    lane = wide // (2 * XLO)
    height = XLO * strip
    cut = total // 2

    def body(core_ref, mine_ref, theirs_ref, *refs):
        out_ref = refs[-1]

        def emit(panel_ref):
            rows = panel_ref[...].reshape(height, total)
            for r in range(YS):
                low, high = refs[2 * r][...], refs[2 * r + 1][...]
                out = jnp.dot(rows[:, :cut], low, preferred_element_type=jnp.float32)
                out += jnp.dot(rows[:, cut:], high, preferred_element_type=jnp.float32)
                out = (out * (1.0 / total)).astype(jnp.bfloat16)
                for xl in range(XLO):
                    for h in range(2):
                        at = (xl * 2 + h) * lane
                        out_ref[0, xl, 2 * r + h] = out[:, at : at + lane]

        pl.when(pl.program_id(0) == 0)(lambda: emit(mine_ref))
        pl.when(pl.program_id(0) == 1)(lambda: emit(theirs_ref))

    def whole(a):
        return pl.BlockSpec(a.shape, lambda k, t, core: (0, 0))

    strips = (XLO, strip, total)
    out = pl.pallas_call(
        body,
        out_shape=jax.ShapeDtypeStruct((2 * CORES, XLO, 2 * YS, height, lane), jnp.bfloat16),
        grid_spec=pltpu.PrefetchScalarGridSpec(
            num_scalar_prefetch=1,
            grid=(CORES, 2),
            in_specs=[
                pl.BlockSpec(strips, lambda k, t, core: (jnp.where(k == 0, t, 1), 0, 0)),
                pl.BlockSpec(strips, lambda k, t, core: (jnp.where(k == 0, 0, t), 0, 0)),
            ]
            + [whole(a) for a in acts],
            out_specs=pl.BlockSpec(
                (1, XLO, 2 * YS, height, lane),
                lambda k, t, core: (t * CORES + jnp.where(k == 0, core[0], 1 - core[0]), 0, 0, 0, 0),
            ),
        ),
        cost_estimate=cost(
            2 * 2 * CORES * height * total * YS * wide,
            2 * (MATES * strip * total + YS * total * wide + MATES * height * 2 * YS * lane),
        ),
        compiler_params=params(),
    )(core, mine, theirs, *acts)
    return out.reshape(MATES, 2 * YS, height, lane)


def place(ys, received):
    _, _, height, lane = received.shape
    slab = MATES * 2 * YS * lane

    def body(ys_ref, in_ref, out_ref):
        for s in range(MATES):
            out_ref[:, s * lane : (s + 1) * lane] = in_ref[s, 0]

    return pl.pallas_call(
        body,
        out_shape=jax.ShapeDtypeStruct((height, slab), jnp.bfloat16),
        grid_spec=pltpu.PrefetchScalarGridSpec(
            num_scalar_prefetch=1,
            grid=(YS, 2),
            in_specs=[
                pl.BlockSpec((MATES, 1, height, lane), lambda r, h, ys: (0, 2 * r + h, 0, 0))
            ],
            out_specs=pl.BlockSpec((height, MATES * lane), lambda r, h, ys: (0, h * YS + ys[r])),
        ),
        cost_estimate=cost(0, 4 * height * slab),
        compiler_params=params(8 * 1024 * 1024),
    )(ys, received)


def per_device(tokens, dec_bias, enc_weight, enc_bias):
    own, width = tokens.shape
    rows, slab = enc_weight.shape
    lane = slab // (2 * CHIPS * CORES * XLO)
    total = own * CHIPS * CORES
    core = lax.axis_index("c")
    xlo = lax.axis_index("xl")
    y = lax.axis_index("y")
    chip = y * 2 + lax.axis_index("xh")
    z = lax.axis_index("z")
    which = jnp.reshape(core, (1,)).astype(jnp.int32)
    ys = lax.rem(jnp.stack([y, y + 3, y + 1, y + 2]), YS).astype(jnp.int32)

    centered = (tokens.astype(jnp.float32) - dec_bias).astype(jnp.bfloat16)
    halves = centered.reshape(own, CHIPS, CORES, rows).transpose(2, 0, 1, 3)
    halves = halves.reshape(CORES, own, CHIPS * rows)
    keep = jnp.where(core == 0, halves[0], halves[1])
    give = jnp.where(core == 0, halves[1], halves[0])
    got = lax.ppermute(give, "c", SWAP)
    mine = jnp.where(core == xlo, keep, got)
    part = own // DEPTH
    mine = lax.dynamic_slice_in_dim(mine, z * part, part, 0)
    near = spread(mine, PLANE, PEERS).reshape(total // DEPTH, CHIPS * rows)
    pieces = [near]
    low = high = near
    for _ in range(DEPTH // 2 - 1):
        low = lax.ppermute(low, "z", shift("z", 1))
        high = lax.ppermute(high, "z", shift("z", -1))
        pieces += [low, high]
    cut = near.shape[0] // 2
    pieces.append(lax.ppermute(low[:cut], "z", shift("z", 1)))
    pieces.append(lax.ppermute(high[cut:], "z", shift("z", -1)))
    batch = collect(jnp.reshape(z, (1,)).astype(jnp.int32), pieces)

    biases = enc_bias.reshape(2, CHIPS, CORES, XLO, lane)
    biases = lax.dynamic_index_in_dim(biases, chip, 1, keepdims=False)
    biases = lax.dynamic_index_in_dim(biases, core, 1, keepdims=False)
    bias_keep = lax.dynamic_index_in_dim(biases, xlo, 1, keepdims=False)
    bias_give = lax.dynamic_index_in_dim(biases, 1 - xlo, 1, keepdims=False)
    bias_got = lax.ppermute(bias_give, "xl", SWAP)
    bias = jnp.where(xlo == 0, jnp.stack([bias_keep, bias_got]), jnp.stack([bias_got, bias_keep]))

    weight = exchange(regroup(enc_weight, lane), PLANE)
    sums, sent = encode(which, batch, weight, lane)
    other = lax.ppermute(sent, "c", SWAP)
    low, high, *turned = finish(sums, other, bias)
    held = jnp.concatenate(turned, axis=1)

    def reach(held, span):
        moved = lax.ppermute(held, "z", [(i, i + span) for i in range(0, DEPTH, 2 * span)])
        return jnp.where(lax.rem(z, 2 * span) == span, moved, held)

    size = MATES // CORES
    forth = [(i, (i + 1) % size) for i in range(size)]
    back = [(i, (i - 1) % size) for i in range(size)]
    held = reach(held, 4)
    below_high = lax.ppermute(high, "y", shift("y", 1))
    above_low = lax.ppermute(low, "y", shift("y", -1))
    held, below_high, above_low = lax.optimization_barrier((held, below_high, above_low))
    held = reach(reach(held, 2), 1)
    below_low = lax.ppermute(low, "y", shift("y", 1))
    above_high = lax.ppermute(high, "y", shift("y", -1))
    held, below_low, above_high = lax.optimization_barrier((held, below_low, above_high))
    left = lax.ppermute(held, LINE, forth)
    right = lax.ppermute(held, LINE, back)
    far_low = lax.ppermute(above_low, "y", shift("y", -1))
    far_high = lax.ppermute(below_high, "y", shift("y", 1))
    right, far_low, far_high = lax.optimization_barrier((right, far_low, far_high))
    over = lax.ppermute(right, LINE, back)
    here = jnp.reshape(lax.axis_index("xh") * XLO + xlo, (1,)).astype(jnp.int32)
    panel = assemble(here, (held, left, right, over), size)
    theirs = lax.ppermute(panel, "c", SWAP)

    acts = (low, high, below_low, below_high, above_low, above_high, far_low, far_high)
    sent = gram(which, panel, theirs, acts)
    return place(ys, exchange(sent, ROW))


def solution(mesh):
    fine = Mesh(mesh.devices.reshape(SIZES), AXES)
    return jax.shard_map(
        per_device,
        mesh=fine,
        in_specs=(P(TOK, None), P(), P(TOK, LATENT), P(LATENT)),
        out_specs=P(TOK, LATENT),
        check_vma=False,
    )
```

```python
import jax
import jax.numpy as jnp
from jax import lax
from jax.experimental import pallas as pl
from jax.experimental.pallas import tpu as pltpu
from jax.sharding import Mesh, PartitionSpec as P

AXES = ("y", "xh", "c", "xl", "z")
SIZES = (4, 2, 2, 2, 8)
PLANE = ("y", "xh", "xl")
ROW = ("xh", "c", "xl")
LINE = ("xh", "xl")
TOK = ("y", "xh", "c")
LATENT = ("xl", "z")
YS, CHIPS, CORES, XLO, DEPTH = 4, 8, 2, 2, 8
PEERS = CHIPS * XLO
MATES = 8
SWAP = [(0, 1), (1, 0)]
VMEM = 60 * 1024 * 1024
ORDER = ((0, 0), (-1, 0), (1, 0), (-2, 0), (2, 0), (-3, 0), (3, 0), (4, 0), (4, 1))


def shift(axis, step):
    size = SIZES[AXES.index(axis)]
    return [(i, (i + step) % size) for i in range(size)]


def params(limit=VMEM):
    return pltpu.CompilerParams(vmem_limit_bytes=limit)


def cost(flops, moved):
    return pl.CostEstimate(flops=flops, bytes_accessed=moved, transcendentals=0)


def exchange(block, axes):
    return lax.all_to_all(block, axes, split_axis=0, concat_axis=0, tiled=True)


def spread(block, axes, count):
    return exchange(jnp.broadcast_to(block[None], (count,) + block.shape), axes)


def regroup(weight, lane):
    rows = weight.shape[0]
    group = 4

    def body(in_ref, out_ref):
        for t in range(group):
            for xl in range(XLO):
                for c in range(CORES):
                    at = ((t * CORES + c) * XLO + xl) * lane
                    to = slice(c * lane, (c + 1) * lane)
                    out_ref[t * XLO + xl, :, to] = in_ref[:, at : at + lane]

    wide = group * CORES * XLO * lane
    steps = CHIPS // group
    return pl.pallas_call(
        body,
        out_shape=jax.ShapeDtypeStruct((PEERS, rows, 2 * CORES * lane), weight.dtype),
        grid=(2, steps),
        in_specs=[pl.BlockSpec((rows, wide), lambda h, t: (0, h * steps + t))],
        out_specs=pl.BlockSpec((group * XLO, rows, CORES * lane), lambda h, t: (t, 0, h)),
        cost_estimate=cost(0, 4 * PEERS * rows * 2 * CORES * lane),
        compiler_params=params(),
    )(weight)


def collect(z, pieces):
    strip, depth = pieces[0].shape
    count = len(pieces)

    def body(z_ref, *refs):
        out_ref, sems = refs[-2:]
        copies = []
        for i, (step, cut) in enumerate(ORDER):
            start = lax.rem(z_ref[0] + step + DEPTH, DEPTH) * strip + cut * (strip // 2)
            at = pl.ds(pl.multiple_of(start, strip // 2), refs[i].shape[0])
            copies.append(pltpu.make_async_copy(refs[i], out_ref.at[at], sems.at[i]))
        for copy in copies:
            copy.start()
        for copy in copies:
            copy.wait()

    return pl.pallas_call(
        body,
        out_shape=jax.ShapeDtypeStruct((DEPTH * strip, depth), pieces[0].dtype),
        in_specs=[pl.BlockSpec(memory_space=pltpu.SMEM)]
        + [pl.BlockSpec(memory_space=pl.ANY)] * count,
        out_specs=pl.BlockSpec(memory_space=pl.ANY),
        scratch_shapes=[pltpu.SemaphoreType.DMA((count,))],
        cost_estimate=cost(0, 4 * DEPTH * strip * depth),
        compiler_params=params(16 * 1024 * 1024),
    )(z, *pieces)


def encode(core, batch, weight, lane):
    total, depth = batch.shape
    _, rows, cols = weight.shape
    wide = XLO * cols
    chunk = total // 2

    def body(core_ref, batch_ref, weight_ref, keep_ref, give_ref, grid, sems):
        slabs = [
            [
                pltpu.make_async_copy(
                    weight_ref.at[t * XLO + xl],
                    grid.at[xl, pl.ds(t * rows, rows)],
                    sems.at[t * XLO + xl],
                )
                for t in range(CHIPS)
            ]
            for xl in range(XLO)
        ]
        xl, i = pl.program_id(0), pl.program_id(1)

        @pl.when((xl == 0) & (i == 0))
        def _():
            for copy in slabs[0] + slabs[1]:
                copy.start()
            for copy in slabs[0]:
                copy.wait()

        @pl.when((xl == 1) & (i == 0))
        def _():
            for copy in slabs[1]:
                copy.wait()

        at = pl.ds(pl.multiple_of(i * chunk, chunk), chunk)
        out = jnp.dot(batch_ref[at], grid[xl], preferred_element_type=jnp.float32)
        for h in range(2):
            a = out[:, 2 * h * lane : (2 * h + 1) * lane]
            b = out[:, (2 * h + 1) * lane : (2 * h + 2) * lane]
            keep_ref[:, h * lane : (h + 1) * lane] = jnp.where(core_ref[0] == 0, a, b)
            give_ref[:, h * lane : (h + 1) * lane] = jnp.where(core_ref[0] == 0, b, a)

    mine = wide // CORES
    block = pl.BlockSpec((chunk, 2 * lane), lambda xl, i: (i, xl))
    return pl.pallas_call(
        body,
        out_shape=(
            jax.ShapeDtypeStruct((total, mine), jnp.float32),
            jax.ShapeDtypeStruct((total, mine), jnp.float32),
        ),
        grid=(XLO, total // chunk),
        in_specs=[
            pl.BlockSpec(memory_space=pltpu.SMEM),
            pl.BlockSpec(memory_space=pltpu.VMEM),
            pl.BlockSpec(memory_space=pl.ANY),
        ],
        out_specs=(block, block),
        scratch_shapes=[
            pltpu.VMEM((XLO, CHIPS * rows, cols), jnp.bfloat16),
            pltpu.SemaphoreType.DMA((PEERS,)),
        ],
        cost_estimate=cost(2 * total * depth * wide, 2 * depth * (total + wide) + 8 * total * mine),
        compiler_params=params(58 * 1024 * 1024),
    )(core, batch, weight)


def finish(sums, other, bias):
    total, wide = sums.shape
    lane = wide // (2 * XLO)
    half = total // 2
    chunk = half // 2

    def body(low_sums, high_sums, low_other, high_other, bias_ref, low_ref, high_ref, *turned):
        refs = ((low_sums, low_other, low_ref), (high_sums, high_other, high_ref))
        for (sums_ref, other_ref, act_ref), turned_ref in zip(refs, turned):
            act = jnp.maximum(sums_ref[...] + other_ref[...] + bias_ref[...], 0.0)
            act_ref[...] = act.astype(jnp.bfloat16)
            turned_ref[...] = act[:, :lane].T.astype(jnp.bfloat16)

    steps = half // chunk
    low = pl.BlockSpec((chunk, wide), lambda i: (i, 0))
    high = pl.BlockSpec((chunk, wide), lambda i: (i + steps, 0))
    turned = pl.BlockSpec((lane, chunk), lambda i: (0, i))
    return pl.pallas_call(
        body,
        out_shape=(jax.ShapeDtypeStruct((half, wide), jnp.bfloat16),) * 2
        + (jax.ShapeDtypeStruct((lane, half), jnp.bfloat16),) * 2,
        grid=(steps,),
        in_specs=[low, high, low, high, pl.BlockSpec((1, wide), lambda i: (0, 0))],
        out_specs=(low, low, turned, turned),
        cost_estimate=cost(0, 10 * total * wide),
        compiler_params=params(8 * 1024 * 1024),
    )(sums, sums, other, other, bias.reshape(1, wide))


def assemble(here, parts, size):
    strip, total = parts[0].shape
    order = (0, -1, 1, 2)

    def body(here_ref, *refs):
        out_ref, sems = refs[-2:]
        copies = []
        for i, step in enumerate(order):
            slot = lax.rem(here_ref[0] + step + size, size)
            copies.append(pltpu.make_async_copy(refs[i], out_ref.at[slot], sems.at[i]))
        for copy in copies:
            copy.start()
        for copy in copies:
            copy.wait()

    return pl.pallas_call(
        body,
        out_shape=jax.ShapeDtypeStruct((size, strip, total), parts[0].dtype),
        in_specs=[pl.BlockSpec(memory_space=pltpu.SMEM)]
        + [pl.BlockSpec(memory_space=pl.ANY)] * len(order),
        out_specs=pl.BlockSpec(memory_space=pl.ANY),
        scratch_shapes=[pltpu.SemaphoreType.DMA((len(order),))],
        cost_estimate=cost(0, 4 * size * strip * total),
        compiler_params=params(16 * 1024 * 1024),
    )(here, *parts)


def gram(core, mine, theirs, acts):
    _, strip, total = mine.shape
    wide = acts[0].shape[1]
    lane = wide // (2 * XLO)
    height = XLO * strip
    cut = total // 2

    def body(core_ref, mine_ref, theirs_ref, *refs):
        out_ref = refs[-1]

        def emit(panel_ref):
            rows = panel_ref[...].reshape(height, total)
            for r in range(YS):
                low, high = refs[2 * r][...], refs[2 * r + 1][...]
                out = jnp.dot(rows[:, :cut], low, preferred_element_type=jnp.float32)
                out += jnp.dot(rows[:, cut:], high, preferred_element_type=jnp.float32)
                out = (out * (1.0 / total)).astype(jnp.bfloat16)
                for xl in range(XLO):
                    for h in range(2):
                        at = (xl * 2 + h) * lane
                        out_ref[0, xl, 2 * r + h] = out[:, at : at + lane]

        pl.when(pl.program_id(0) == 0)(lambda: emit(mine_ref))
        pl.when(pl.program_id(0) == 1)(lambda: emit(theirs_ref))

    def whole(a):
        return pl.BlockSpec(a.shape, lambda k, t, core: (0, 0))

    strips = (XLO, strip, total)
    out = pl.pallas_call(
        body,
        out_shape=jax.ShapeDtypeStruct((2 * CORES, XLO, 2 * YS, height, lane), jnp.bfloat16),
        grid_spec=pltpu.PrefetchScalarGridSpec(
            num_scalar_prefetch=1,
            grid=(CORES, 2),
            in_specs=[
                pl.BlockSpec(strips, lambda k, t, core: (jnp.where(k == 0, t, 1), 0, 0)),
                pl.BlockSpec(strips, lambda k, t, core: (jnp.where(k == 0, 0, t), 0, 0)),
            ]
            + [whole(a) for a in acts],
            out_specs=pl.BlockSpec(
                (1, XLO, 2 * YS, height, lane),
                lambda k, t, core: (t * CORES + jnp.where(k == 0, core[0], 1 - core[0]), 0, 0, 0, 0),
            ),
        ),
        cost_estimate=cost(
            2 * 2 * CORES * height * total * YS * wide,
            2 * (MATES * strip * total + YS * total * wide + MATES * height * 2 * YS * lane),
        ),
        compiler_params=params(20 * 1024 * 1024),
    )(core, mine, theirs, *acts)
    return out.reshape(MATES, 2 * YS, height, lane)


def place(ys, received):
    _, _, height, lane = received.shape
    slab = MATES * 2 * YS * lane

    def body(ys_ref, in_ref, out_ref):
        for s in range(MATES):
            out_ref[:, s * lane : (s + 1) * lane] = in_ref[s, 0]

    return pl.pallas_call(
        body,
        out_shape=jax.ShapeDtypeStruct((height, slab), jnp.bfloat16),
        grid_spec=pltpu.PrefetchScalarGridSpec(
            num_scalar_prefetch=1,
            grid=(YS, 2),
            in_specs=[
                pl.BlockSpec((MATES, 1, height, lane), lambda r, h, ys: (0, 2 * r + h, 0, 0))
            ],
            out_specs=pl.BlockSpec((height, MATES * lane), lambda r, h, ys: (0, h * YS + ys[r])),
        ),
        cost_estimate=cost(0, 4 * height * slab),
        compiler_params=params(8 * 1024 * 1024),
    )(ys, received)


def per_device(tokens, dec_bias, enc_weight, enc_bias):
    own, width = tokens.shape
    rows, slab = enc_weight.shape
    lane = slab // (2 * CHIPS * CORES * XLO)
    total = own * CHIPS * CORES
    core = lax.axis_index("c")
    xlo = lax.axis_index("xl")
    y = lax.axis_index("y")
    chip = y * 2 + lax.axis_index("xh")
    z = lax.axis_index("z")
    which = jnp.reshape(core, (1,)).astype(jnp.int32)
    ys = lax.rem(jnp.stack([y, y + 3, y + 1, y + 2]), YS).astype(jnp.int32)

    centered = (tokens.astype(jnp.float32) - dec_bias).astype(jnp.bfloat16)
    halves = centered.reshape(own, CHIPS, CORES, rows).transpose(2, 0, 1, 3)
    halves = halves.reshape(CORES, own, CHIPS * rows)
    keep = jnp.where(core == 0, halves[0], halves[1])
    give = jnp.where(core == 0, halves[1], halves[0])
    got = lax.ppermute(give, "c", SWAP)
    mine = jnp.where(core == xlo, keep, got)
    part = own // DEPTH
    mine = lax.dynamic_slice_in_dim(mine, z * part, part, 0)
    near = spread(mine, PLANE, PEERS).reshape(total // DEPTH, CHIPS * rows)
    pieces = [near]
    low = high = near
    for _ in range(DEPTH // 2 - 1):
        low = lax.ppermute(low, "z", shift("z", 1))
        high = lax.ppermute(high, "z", shift("z", -1))
        pieces += [low, high]
    cut = near.shape[0] // 2
    pieces.append(lax.ppermute(low[:cut], "z", shift("z", 1)))
    pieces.append(lax.ppermute(high[cut:], "z", shift("z", -1)))
    batch = collect(jnp.reshape(z, (1,)).astype(jnp.int32), pieces)

    biases = enc_bias.reshape(2, CHIPS, CORES, XLO, lane)
    biases = lax.dynamic_index_in_dim(biases, chip, 1, keepdims=False)
    biases = lax.dynamic_index_in_dim(biases, core, 1, keepdims=False)
    bias_keep = lax.dynamic_index_in_dim(biases, xlo, 1, keepdims=False)
    bias_give = lax.dynamic_index_in_dim(biases, 1 - xlo, 1, keepdims=False)
    bias_got = lax.ppermute(bias_give, "xl", SWAP)
    bias = jnp.where(xlo == 0, jnp.stack([bias_keep, bias_got]), jnp.stack([bias_got, bias_keep]))

    weight = exchange(regroup(enc_weight, lane), PLANE)
    sums, sent = encode(which, batch, weight, lane)
    other = lax.ppermute(sent, "c", SWAP)
    low, high, *turned = finish(sums, other, bias)
    held = jnp.concatenate(turned, axis=1)

    def reach(held, step, sources):
        up = lax.ppermute(held, "z", [(i, (i + step) % DEPTH) for i in sources[0]])
        down = lax.ppermute(held, "z", [(i, (i - step) % DEPTH) for i in sources[1]])
        for moved, origins, sign in ((up, sources[0], 1), (down, sources[1], -1)):
            for i in origins:
                held = jnp.where(z == (i + sign * step) % DEPTH, moved, held)
        return held

    size = MATES // CORES
    forth = [(i, (i + 1) % size) for i in range(size)]
    back = [(i, (i - 1) % size) for i in range(size)]
    held = reach(held, 3, ((0,), (0,)))
    below_high = lax.ppermute(high, "y", shift("y", 1))
    above_low = lax.ppermute(low, "y", shift("y", -1))
    held, below_high, above_low = lax.optimization_barrier((held, below_high, above_low))
    held = reach(held, 1, ((0, 3, 5), (0, 3)))
    below_low = lax.ppermute(low, "y", shift("y", 1))
    above_high = lax.ppermute(high, "y", shift("y", -1))
    held, below_low, above_high = lax.optimization_barrier((held, below_low, above_high))
    left = lax.ppermute(held, LINE, forth)
    right = lax.ppermute(held, LINE, back)
    far_low = lax.ppermute(above_low, "y", shift("y", -1))
    far_high = lax.ppermute(below_high, "y", shift("y", 1))
    over = lax.ppermute(right, LINE, back)
    over, far_low, far_high = lax.optimization_barrier((over, far_low, far_high))
    here = jnp.reshape(lax.axis_index("xh") * XLO + xlo, (1,)).astype(jnp.int32)
    panel = assemble(here, (held, left, right, over), size)
    theirs = lax.ppermute(panel, "c", SWAP)

    acts = (low, high, below_low, below_high, above_low, above_high, far_low, far_high)
    sent, ys = lax.optimization_barrier((gram(which, panel, theirs, acts), ys))
    return place(ys, exchange(sent, ROW))


def solution(mesh):
    fine = Mesh(mesh.devices.reshape(SIZES), AXES)
    return jax.shard_map(
        per_device,
        mesh=fine,
        in_specs=(P(TOK, None), P(), P(TOK, LATENT), P(LATENT)),
        out_specs=P(TOK, LATENT),
        check_vma=False,
    )
```

```python
import jax
import jax.numpy as jnp
from jax import lax
from jax.experimental import pallas as pl
from jax.experimental.pallas import tpu as pltpu
from jax.sharding import Mesh, PartitionSpec as P

AXES = ("y", "xh", "c", "xl", "z")
SIZES = (4, 2, 2, 2, 8)
PLANE = ("y", "xh", "xl")
ROW = ("xh", "c", "xl")
LINE = ("xh", "xl")
TOK = ("y", "xh", "c")
LATENT = ("xl", "z")
YS, CHIPS, CORES, XLO, DEPTH = 4, 8, 2, 2, 8
PEERS = CHIPS * XLO
MATES = 8
SWAP = [(0, 1), (1, 0)]
VMEM = 60 * 1024 * 1024
ORDER = ((0, 0), (-1, 0), (1, 0), (-2, 0), (2, 0), (-3, 0), (3, 0), (4, 0), (4, 1))


def shift(axis, step):
    size = SIZES[AXES.index(axis)]
    return [(i, (i + step) % size) for i in range(size)]


def params(limit=VMEM):
    return pltpu.CompilerParams(vmem_limit_bytes=limit)


def cost(flops, moved):
    return pl.CostEstimate(flops=flops, bytes_accessed=moved, transcendentals=0)


def exchange(block, axes):
    return lax.all_to_all(block, axes, split_axis=0, concat_axis=0, tiled=True)


def spread(block, axes, count):
    return exchange(jnp.broadcast_to(block[None], (count,) + block.shape), axes)


def regroup(weight, lane):
    rows = weight.shape[0]
    group = 4

    def body(in_ref, out_ref):
        for t in range(group):
            for xl in range(XLO):
                for c in range(CORES):
                    at = ((t * CORES + c) * XLO + xl) * lane
                    to = slice(c * lane, (c + 1) * lane)
                    out_ref[t * XLO + xl, :, to] = in_ref[:, at : at + lane]

    wide = group * CORES * XLO * lane
    steps = CHIPS // group
    return pl.pallas_call(
        body,
        out_shape=jax.ShapeDtypeStruct((PEERS, rows, 2 * CORES * lane), weight.dtype),
        grid=(2, steps),
        in_specs=[pl.BlockSpec((rows, wide), lambda h, t: (0, h * steps + t))],
        out_specs=pl.BlockSpec((group * XLO, rows, CORES * lane), lambda h, t: (t, 0, h)),
        cost_estimate=cost(0, 4 * PEERS * rows * 2 * CORES * lane),
        compiler_params=params(),
    )(weight)


def collect(z, pieces):
    strip, depth = pieces[0].shape
    count = len(pieces)

    def body(z_ref, *refs):
        out_ref, sems = refs[-2:]
        copies = []
        for i, (step, cut) in enumerate(ORDER):
            start = lax.rem(z_ref[0] + step + DEPTH, DEPTH) * strip + cut * (strip // 2)
            at = pl.ds(pl.multiple_of(start, strip // 2), refs[i].shape[0])
            copies.append(pltpu.make_async_copy(refs[i], out_ref.at[at], sems.at[i]))
        for copy in copies:
            copy.start()
        for copy in copies:
            copy.wait()

    return pl.pallas_call(
        body,
        out_shape=jax.ShapeDtypeStruct((DEPTH * strip, depth), pieces[0].dtype),
        in_specs=[pl.BlockSpec(memory_space=pltpu.SMEM)]
        + [pl.BlockSpec(memory_space=pl.ANY)] * count,
        out_specs=pl.BlockSpec(memory_space=pl.ANY),
        scratch_shapes=[pltpu.SemaphoreType.DMA((count,))],
        cost_estimate=cost(0, 4 * DEPTH * strip * depth),
        compiler_params=params(16 * 1024 * 1024),
    )(z, *pieces)


def encode(core, batch, weight, lane):
    total, depth = batch.shape
    _, rows, cols = weight.shape
    wide = XLO * cols
    chunk = total // 2

    def body(core_ref, batch_ref, weight_ref, keep_ref, give_ref, grid, sems):
        slabs = [
            [
                pltpu.make_async_copy(
                    weight_ref.at[t * XLO + xl],
                    grid.at[xl, pl.ds(t * rows, rows)],
                    sems.at[t * XLO + xl],
                )
                for t in range(CHIPS)
            ]
            for xl in range(XLO)
        ]
        xl, i = pl.program_id(0), pl.program_id(1)

        @pl.when((xl == 0) & (i == 0))
        def _():
            for copy in slabs[0] + slabs[1]:
                copy.start()
            for copy in slabs[0]:
                copy.wait()

        @pl.when((xl == 1) & (i == 0))
        def _():
            for copy in slabs[1]:
                copy.wait()

        at = pl.ds(pl.multiple_of(i * chunk, chunk), chunk)
        out = jnp.dot(batch_ref[at], grid[xl], preferred_element_type=jnp.float32)
        for h in range(2):
            a = out[:, 2 * h * lane : (2 * h + 1) * lane]
            b = out[:, (2 * h + 1) * lane : (2 * h + 2) * lane]
            keep_ref[:, h * lane : (h + 1) * lane] = jnp.where(core_ref[0] == 0, a, b)
            give_ref[:, h * lane : (h + 1) * lane] = jnp.where(core_ref[0] == 0, b, a)

    mine = wide // CORES
    block = pl.BlockSpec((chunk, 2 * lane), lambda xl, i: (i, xl))
    return pl.pallas_call(
        body,
        out_shape=(
            jax.ShapeDtypeStruct((total, mine), jnp.float32),
            jax.ShapeDtypeStruct((total, mine), jnp.float32),
        ),
        grid=(XLO, total // chunk),
        in_specs=[
            pl.BlockSpec(memory_space=pltpu.SMEM),
            pl.BlockSpec(memory_space=pltpu.VMEM),
            pl.BlockSpec(memory_space=pl.ANY),
        ],
        out_specs=(block, block),
        scratch_shapes=[
            pltpu.VMEM((XLO, CHIPS * rows, cols), jnp.bfloat16),
            pltpu.SemaphoreType.DMA((PEERS,)),
        ],
        cost_estimate=cost(2 * total * depth * wide, 2 * depth * (total + wide) + 8 * total * mine),
        compiler_params=params(58 * 1024 * 1024),
    )(core, batch, weight)


def finish(sums, other, bias):
    total, wide = sums.shape
    lane = wide // (2 * XLO)
    half = total // 2
    chunk = half // 2

    def body(low_sums, high_sums, low_other, high_other, bias_ref, low_ref, high_ref, *turned):
        refs = ((low_sums, low_other, low_ref), (high_sums, high_other, high_ref))
        for (sums_ref, other_ref, act_ref), turned_ref in zip(refs, turned):
            act = jnp.maximum(sums_ref[...] + other_ref[...] + bias_ref[...], 0.0)
            act_ref[...] = act.astype(jnp.bfloat16)
            turned_ref[...] = act[:, :lane].T.astype(jnp.bfloat16)

    steps = half // chunk
    low = pl.BlockSpec((chunk, wide), lambda i: (i, 0))
    high = pl.BlockSpec((chunk, wide), lambda i: (i + steps, 0))
    turned = pl.BlockSpec((lane, chunk), lambda i: (0, i))
    return pl.pallas_call(
        body,
        out_shape=(jax.ShapeDtypeStruct((half, wide), jnp.bfloat16),) * 2
        + (jax.ShapeDtypeStruct((lane, half), jnp.bfloat16),) * 2,
        grid=(steps,),
        in_specs=[low, high, low, high, pl.BlockSpec((1, wide), lambda i: (0, 0))],
        out_specs=(low, low, turned, turned),
        cost_estimate=cost(0, 10 * total * wide),
        compiler_params=params(8 * 1024 * 1024),
    )(sums, sums, other, other, bias.reshape(1, wide))


def assemble(here, parts, size):
    strip, total = parts[0].shape
    order = (0, -1, 1, 2)

    def body(here_ref, *refs):
        out_ref, sems = refs[-2:]
        copies = []
        for i, step in enumerate(order):
            slot = lax.rem(here_ref[0] + step + size, size)
            copies.append(pltpu.make_async_copy(refs[i], out_ref.at[slot], sems.at[i]))
        for copy in copies:
            copy.start()
        for copy in copies:
            copy.wait()

    return pl.pallas_call(
        body,
        out_shape=jax.ShapeDtypeStruct((size, strip, total), parts[0].dtype),
        in_specs=[pl.BlockSpec(memory_space=pltpu.SMEM)]
        + [pl.BlockSpec(memory_space=pl.ANY)] * len(order),
        out_specs=pl.BlockSpec(memory_space=pl.ANY),
        scratch_shapes=[pltpu.SemaphoreType.DMA((len(order),))],
        cost_estimate=cost(0, 4 * size * strip * total),
        compiler_params=params(16 * 1024 * 1024),
    )(here, *parts)


def gram(core, mine, theirs, acts):
    _, strip, total = mine.shape
    wide = acts[0].shape[1]
    lane = wide // (2 * XLO)
    height = XLO * strip
    cut = total // 2

    def body(core_ref, mine_ref, theirs_ref, *refs):
        out_ref = refs[-1]

        def emit(panel_ref):
            rows = panel_ref[...].reshape(height, total)
            for r in range(YS):
                low, high = refs[2 * r][...], refs[2 * r + 1][...]
                out = jnp.dot(rows[:, :cut], low, preferred_element_type=jnp.float32)
                out += jnp.dot(rows[:, cut:], high, preferred_element_type=jnp.float32)
                out = (out * (1.0 / total)).astype(jnp.bfloat16)
                for xl in range(XLO):
                    for h in range(2):
                        at = (xl * 2 + h) * lane
                        out_ref[0, xl, 2 * r + h] = out[:, at : at + lane]

        pl.when(pl.program_id(0) == 0)(lambda: emit(mine_ref))
        pl.when(pl.program_id(0) == 1)(lambda: emit(theirs_ref))

    def whole(a):
        return pl.BlockSpec(a.shape, lambda k, t, core: (0, 0))

    strips = (XLO, strip, total)
    out = pl.pallas_call(
        body,
        out_shape=jax.ShapeDtypeStruct((2 * CORES, XLO, 2 * YS, height, lane), jnp.bfloat16),
        grid_spec=pltpu.PrefetchScalarGridSpec(
            num_scalar_prefetch=1,
            grid=(CORES, 2),
            in_specs=[
                pl.BlockSpec(strips, lambda k, t, core: (jnp.where(k == 0, t, 1), 0, 0)),
                pl.BlockSpec(strips, lambda k, t, core: (jnp.where(k == 0, 0, t), 0, 0)),
            ]
            + [whole(a) for a in acts],
            out_specs=pl.BlockSpec(
                (1, XLO, 2 * YS, height, lane),
                lambda k, t, core: (t * CORES + jnp.where(k == 0, core[0], 1 - core[0]), 0, 0, 0, 0),
            ),
        ),
        cost_estimate=cost(
            2 * 2 * CORES * height * total * YS * wide,
            2 * (MATES * strip * total + YS * total * wide + MATES * height * 2 * YS * lane),
        ),
        compiler_params=params(57 * 1024 * 1024),
    )(core, mine, theirs, *acts)
    return out.reshape(MATES, 2 * YS, height, lane)


def place(ys, received):
    _, strips, height, lane = received.shape
    wide = MATES * lane

    def body(ys_ref, in_ref, out_ref, staged, sems):
        copies = []
        for i in range(strips):
            for s in range(MATES):
                staged[i, :, s * lane : (s + 1) * lane] = in_ref[s, i]
            start = ((i % 2) * YS + ys_ref[i // 2]) * wide
            to = out_ref.at[:, pl.ds(pl.multiple_of(start, lane), wide)]
            copies.append(pltpu.make_async_copy(staged.at[i], to, sems.at[i]))
            copies[-1].start()
        for copy in copies:
            copy.wait()

    return pl.pallas_call(
        body,
        out_shape=jax.ShapeDtypeStruct((height, strips * wide), jnp.bfloat16),
        in_specs=[
            pl.BlockSpec(memory_space=pltpu.SMEM),
            pl.BlockSpec(memory_space=pltpu.VMEM),
        ],
        out_specs=pl.BlockSpec(memory_space=pl.ANY),
        scratch_shapes=[
            pltpu.VMEM((strips, height, wide), jnp.bfloat16),
            pltpu.SemaphoreType.DMA((strips,)),
        ],
        cost_estimate=cost(0, 4 * height * strips * wide),
        compiler_params=params(16 * 1024 * 1024),
    )(ys, received)


def per_device(tokens, dec_bias, enc_weight, enc_bias):
    own, width = tokens.shape
    rows, slab = enc_weight.shape
    lane = slab // (2 * CHIPS * CORES * XLO)
    total = own * CHIPS * CORES
    core = lax.axis_index("c")
    xlo = lax.axis_index("xl")
    y = lax.axis_index("y")
    chip = y * 2 + lax.axis_index("xh")
    z = lax.axis_index("z")
    which = jnp.reshape(core, (1,)).astype(jnp.int32)
    ys = lax.rem(jnp.stack([y, y + 3, y + 1, y + 2]), YS).astype(jnp.int32)

    centered = (tokens.astype(jnp.float32) - dec_bias).astype(jnp.bfloat16)
    halves = centered.reshape(own, CHIPS, CORES, rows).transpose(2, 0, 1, 3)
    halves = halves.reshape(CORES, own, CHIPS * rows)
    keep = jnp.where(core == 0, halves[0], halves[1])
    give = jnp.where(core == 0, halves[1], halves[0])
    got = lax.ppermute(give, "c", SWAP)
    mine = jnp.where(core == xlo, keep, got)
    part = own // DEPTH
    mine = lax.dynamic_slice_in_dim(mine, z * part, part, 0)
    near = spread(mine, PLANE, PEERS).reshape(total // DEPTH, CHIPS * rows)
    pieces = [near]
    low = high = near
    for _ in range(DEPTH // 2 - 1):
        low = lax.ppermute(low, "z", shift("z", 1))
        high = lax.ppermute(high, "z", shift("z", -1))
        pieces += [low, high]
    cut = near.shape[0] // 2
    pieces.append(lax.ppermute(low[:cut], "z", shift("z", 1)))
    pieces.append(lax.ppermute(high[cut:], "z", shift("z", -1)))
    batch = collect(jnp.reshape(z, (1,)).astype(jnp.int32), pieces)

    biases = enc_bias.reshape(2, CHIPS, CORES, XLO, lane)
    biases = lax.dynamic_index_in_dim(biases, chip, 1, keepdims=False)
    biases = lax.dynamic_index_in_dim(biases, core, 1, keepdims=False)
    bias_keep = lax.dynamic_index_in_dim(biases, xlo, 1, keepdims=False)
    bias_give = lax.dynamic_index_in_dim(biases, 1 - xlo, 1, keepdims=False)
    bias_got = lax.ppermute(bias_give, "xl", SWAP)
    bias = jnp.where(xlo == 0, jnp.stack([bias_keep, bias_got]), jnp.stack([bias_got, bias_keep]))

    weight = exchange(regroup(enc_weight, lane), PLANE)
    sums, sent = encode(which, batch, weight, lane)
    other = lax.ppermute(sent, "c", SWAP)
    low, high, *turned = finish(sums, other, bias)
    held = jnp.concatenate(turned, axis=1)

    def reach(held, step, sources):
        up = lax.ppermute(held, "z", [(i, (i + step) % DEPTH) for i in sources[0]])
        down = lax.ppermute(held, "z", [(i, (i - step) % DEPTH) for i in sources[1]])
        for moved, origins, sign in ((up, sources[0], 1), (down, sources[1], -1)):
            for i in origins:
                held = jnp.where(z == (i + sign * step) % DEPTH, moved, held)
        return held

    size = MATES // CORES
    forth = [(i, (i + 1) % size) for i in range(size)]
    back = [(i, (i - 1) % size) for i in range(size)]
    held = reach(held, 3, ((0,), (0,)))
    below_high = lax.ppermute(high, "y", shift("y", 1))
    above_low = lax.ppermute(low, "y", shift("y", -1))
    held, below_high, above_low = lax.optimization_barrier((held, below_high, above_low))
    held = reach(held, 1, ((0, 3, 5), (0, 3)))
    below_low = lax.ppermute(low, "y", shift("y", 1))
    above_high = lax.ppermute(high, "y", shift("y", -1))
    held, below_low, above_high = lax.optimization_barrier((held, below_low, above_high))
    left = lax.ppermute(held, LINE, forth)
    right = lax.ppermute(held, LINE, back)
    far_low = lax.ppermute(above_low, "y", shift("y", -1))
    far_high = lax.ppermute(below_high, "y", shift("y", 1))
    over = lax.ppermute(held, LINE, [(i, (i + 2) % size) for i in range(size)])
    over, far_low, far_high = lax.optimization_barrier((over, far_low, far_high))
    here = jnp.reshape(lax.axis_index("xh") * XLO + xlo, (1,)).astype(jnp.int32)
    panel = assemble(here, (held, left, right, over), size)
    theirs = lax.ppermute(panel, "c", SWAP)

    acts = (low, high, below_low, below_high, above_low, above_high, far_low, far_high)
    sent, ys = lax.optimization_barrier((gram(which, panel, theirs, acts), ys))
    return place(ys, exchange(sent, ROW))


def solution(mesh):
    fine = Mesh(mesh.devices.reshape(SIZES), AXES)
    return jax.shard_map(
        per_device,
        mesh=fine,
        in_specs=(P(TOK, None), P(), P(TOK, LATENT), P(LATENT)),
        out_specs=P(TOK, LATENT),
        check_vma=False,
    )
```

```python
import jax
import jax.numpy as jnp
from jax import lax
from jax.experimental import pallas as pl
from jax.experimental.pallas import tpu as pltpu
from jax.sharding import Mesh, PartitionSpec as P

AXES = ("y", "xh", "c", "xl", "z")
SIZES = (4, 2, 2, 2, 8)
PLANE = ("y", "xh", "xl")
ROW = ("xh", "c", "xl")
LINE = ("xh", "xl")
TOK = ("y", "xh", "c")
LATENT = ("xl", "z")
YS, CHIPS, CORES, XLO, DEPTH = 4, 8, 2, 2, 8
PEERS = CHIPS * XLO
MATES = 8
SWAP = [(0, 1), (1, 0)]
VMEM = 60 * 1024 * 1024
ORDER = ((0, 0), (-1, 0), (1, 0), (-2, 0), (2, 0), (-3, 0), (3, 0), (4, 0), (4, 1))


def shift(axis, step):
    size = SIZES[AXES.index(axis)]
    return [(i, (i + step) % size) for i in range(size)]


def params(limit=VMEM):
    return pltpu.CompilerParams(vmem_limit_bytes=limit)


def cost(flops, moved):
    return pl.CostEstimate(flops=flops, bytes_accessed=moved, transcendentals=0)


def exchange(block, axes):
    return lax.all_to_all(block, axes, split_axis=0, concat_axis=0, tiled=True)


def spread(block, axes, count):
    return exchange(jnp.broadcast_to(block[None], (count,) + block.shape), axes)


def regroup(weight, lane):
    rows = weight.shape[0]
    group = 4

    def body(in_ref, out_ref):
        for t in range(group):
            for xl in range(XLO):
                for c in range(CORES):
                    at = ((t * CORES + c) * XLO + xl) * lane
                    to = slice(c * lane, (c + 1) * lane)
                    out_ref[t * XLO + xl, :, to] = in_ref[:, at : at + lane]

    wide = group * CORES * XLO * lane
    steps = CHIPS // group
    return pl.pallas_call(
        body,
        out_shape=jax.ShapeDtypeStruct((PEERS, rows, 2 * CORES * lane), weight.dtype),
        grid=(2, steps),
        in_specs=[pl.BlockSpec((rows, wide), lambda h, t: (0, h * steps + t))],
        out_specs=pl.BlockSpec((group * XLO, rows, CORES * lane), lambda h, t: (t, 0, h)),
        cost_estimate=cost(0, 4 * PEERS * rows * 2 * CORES * lane),
        compiler_params=params(),
    )(weight)


def collect(z, pieces):
    strip, depth = pieces[0].shape
    count = len(pieces)

    def body(z_ref, *refs):
        out_ref, sems = refs[-2:]
        copies = []
        for i, (step, cut) in enumerate(ORDER):
            start = lax.rem(z_ref[0] + step + DEPTH, DEPTH) * strip + cut * (strip // 2)
            at = pl.ds(pl.multiple_of(start, strip // 2), refs[i].shape[0])
            copies.append(pltpu.make_async_copy(refs[i], out_ref.at[at], sems.at[i]))
        for copy in copies:
            copy.start()
        for copy in copies:
            copy.wait()

    return pl.pallas_call(
        body,
        out_shape=jax.ShapeDtypeStruct((DEPTH * strip, depth), pieces[0].dtype),
        in_specs=[pl.BlockSpec(memory_space=pltpu.SMEM)]
        + [pl.BlockSpec(memory_space=pl.ANY)] * count,
        out_specs=pl.BlockSpec(memory_space=pl.ANY),
        scratch_shapes=[pltpu.SemaphoreType.DMA((count,))],
        cost_estimate=cost(0, 4 * DEPTH * strip * depth),
        compiler_params=params(16 * 1024 * 1024),
    )(z, *pieces)


def encode(core, batch, weight, lane):
    total, depth = batch.shape
    _, rows, cols = weight.shape
    wide = XLO * cols
    chunk = total // 2

    def body(core_ref, batch_ref, weight_ref, keep_ref, give_ref, grid, sems):
        slabs = [
            [
                pltpu.make_async_copy(
                    weight_ref.at[t * XLO + xl],
                    grid.at[xl, pl.ds(t * rows, rows)],
                    sems.at[t * XLO + xl],
                )
                for t in range(CHIPS)
            ]
            for xl in range(XLO)
        ]
        xl, i = pl.program_id(0), pl.program_id(1)

        @pl.when((xl == 0) & (i == 0))
        def _():
            for copy in slabs[0]:
                copy.start()
            for copy in slabs[0]:
                copy.wait()
            for copy in slabs[1]:
                copy.start()

        @pl.when((xl == 1) & (i == 0))
        def _():
            for copy in slabs[1]:
                copy.wait()

        at = pl.ds(pl.multiple_of(i * chunk, chunk), chunk)
        out = jnp.dot(batch_ref[at], grid[xl], preferred_element_type=jnp.float32)
        for h in range(2):
            a = out[:, 2 * h * lane : (2 * h + 1) * lane]
            b = out[:, (2 * h + 1) * lane : (2 * h + 2) * lane]
            keep_ref[:, h * lane : (h + 1) * lane] = jnp.where(core_ref[0] == 0, a, b)
            give_ref[:, h * lane : (h + 1) * lane] = jnp.where(core_ref[0] == 0, b, a)

    mine = wide // CORES
    block = pl.BlockSpec((chunk, 2 * lane), lambda xl, i: (i, xl))
    return pl.pallas_call(
        body,
        out_shape=(
            jax.ShapeDtypeStruct((total, mine), jnp.float32),
            jax.ShapeDtypeStruct((total, mine), jnp.float32),
        ),
        grid=(XLO, total // chunk),
        in_specs=[
            pl.BlockSpec(memory_space=pltpu.SMEM),
            pl.BlockSpec(memory_space=pltpu.VMEM),
            pl.BlockSpec(memory_space=pl.ANY),
        ],
        out_specs=(block, block),
        scratch_shapes=[
            pltpu.VMEM((XLO, CHIPS * rows, cols), jnp.bfloat16),
            pltpu.SemaphoreType.DMA((PEERS,)),
        ],
        cost_estimate=cost(2 * total * depth * wide, 2 * depth * (total + wide) + 8 * total * mine),
        compiler_params=params(58 * 1024 * 1024),
    )(core, batch, weight)


def finish(sums, other, bias):
    total, wide = sums.shape
    lane = wide // (2 * XLO)
    half = total // 2
    chunk = half // 2

    def body(low_sums, high_sums, low_other, high_other, bias_ref, low_ref, high_ref, *turned):
        refs = ((low_sums, low_other, low_ref), (high_sums, high_other, high_ref))
        for (sums_ref, other_ref, act_ref), turned_ref in zip(refs, turned):
            act = jnp.maximum(sums_ref[...] + other_ref[...] + bias_ref[...], 0.0)
            act_ref[...] = act.astype(jnp.bfloat16)
            turned_ref[...] = act[:, :lane].T.astype(jnp.bfloat16)

    steps = half // chunk
    low = pl.BlockSpec((chunk, wide), lambda i: (i, 0))
    high = pl.BlockSpec((chunk, wide), lambda i: (i + steps, 0))
    turned = pl.BlockSpec((lane, chunk), lambda i: (0, i))
    return pl.pallas_call(
        body,
        out_shape=(jax.ShapeDtypeStruct((half, wide), jnp.bfloat16),) * 2
        + (jax.ShapeDtypeStruct((lane, half), jnp.bfloat16),) * 2,
        grid=(steps,),
        in_specs=[low, high, low, high, pl.BlockSpec((1, wide), lambda i: (0, 0))],
        out_specs=(low, low, turned, turned),
        cost_estimate=cost(0, 10 * total * wide),
        compiler_params=params(8 * 1024 * 1024),
    )(sums, sums, other, other, bias.reshape(1, wide))


def assemble(here, parts, size):
    strip, total = parts[0].shape
    order = (0, -1, 1, 2)

    def body(here_ref, *refs):
        out_ref, sems = refs[-2:]
        copies = []
        for i, step in enumerate(order):
            slot = lax.rem(here_ref[0] + step + size, size)
            copies.append(pltpu.make_async_copy(refs[i], out_ref.at[slot], sems.at[i]))
        for copy in copies:
            copy.start()
        for copy in copies:
            copy.wait()

    return pl.pallas_call(
        body,
        out_shape=jax.ShapeDtypeStruct((size, strip, total), parts[0].dtype),
        in_specs=[pl.BlockSpec(memory_space=pltpu.SMEM)]
        + [pl.BlockSpec(memory_space=pl.ANY)] * len(order),
        out_specs=pl.BlockSpec(memory_space=pl.ANY),
        scratch_shapes=[pltpu.SemaphoreType.DMA((len(order),))],
        cost_estimate=cost(0, 4 * size * strip * total),
        compiler_params=params(16 * 1024 * 1024),
    )(here, *parts)


def gram(core, mine, theirs, acts):
    _, strip, total = mine.shape
    wide = acts[0].shape[1]
    lane = wide // (2 * XLO)
    height = XLO * strip
    cut = total // 2

    def body(core_ref, mine_ref, theirs_ref, *refs):
        out_ref = refs[-1]

        def emit(panel_ref):
            rows = panel_ref[...].reshape(height, total)
            for r in range(YS):
                low, high = refs[2 * r][...], refs[2 * r + 1][...]
                out = jnp.dot(rows[:, :cut], low, preferred_element_type=jnp.float32)
                out += jnp.dot(rows[:, cut:], high, preferred_element_type=jnp.float32)
                out = (out * (1.0 / total)).astype(jnp.bfloat16)
                for xl in range(XLO):
                    for h in range(2):
                        at = (xl * 2 + h) * lane
                        out_ref[0, xl, 2 * r + h] = out[:, at : at + lane]

        pl.when(pl.program_id(0) == 0)(lambda: emit(mine_ref))
        pl.when(pl.program_id(0) == 1)(lambda: emit(theirs_ref))

    def whole(a):
        return pl.BlockSpec(a.shape, lambda k, t, core: (0, 0))

    strips = (XLO, strip, total)
    out = pl.pallas_call(
        body,
        out_shape=jax.ShapeDtypeStruct((2 * CORES, XLO, 2 * YS, height, lane), jnp.bfloat16),
        grid_spec=pltpu.PrefetchScalarGridSpec(
            num_scalar_prefetch=1,
            grid=(CORES, 2),
            in_specs=[
                pl.BlockSpec(strips, lambda k, t, core: (jnp.where(k == 0, t, 1), 0, 0)),
                pl.BlockSpec(strips, lambda k, t, core: (jnp.where(k == 0, 0, t), 0, 0)),
            ]
            + [whole(a) for a in acts],
            out_specs=pl.BlockSpec(
                (1, XLO, 2 * YS, height, lane),
                lambda k, t, core: (t * CORES + jnp.where(k == 0, core[0], 1 - core[0]), 0, 0, 0, 0),
            ),
        ),
        cost_estimate=cost(
            2 * 2 * CORES * height * total * YS * wide,
            2 * (MATES * strip * total + YS * total * wide + MATES * height * 2 * YS * lane),
        ),
        compiler_params=params(57 * 1024 * 1024),
    )(core, mine, theirs, *acts)
    return out.reshape(MATES, 2 * YS, height, lane)


def place(ys, received):
    _, strips, height, lane = received.shape
    wide = MATES * lane

    def body(ys_ref, in_ref, out_ref, staged, sems):
        copies = []
        for i in range(strips):
            for s in range(MATES):
                staged[i, :, s * lane : (s + 1) * lane] = in_ref[s, i]
            start = ((i % 2) * YS + ys_ref[i // 2]) * wide
            to = out_ref.at[:, pl.ds(pl.multiple_of(start, lane), wide)]
            copies.append(pltpu.make_async_copy(staged.at[i], to, sems.at[i]))
            copies[-1].start()
        for copy in copies:
            copy.wait()

    return pl.pallas_call(
        body,
        out_shape=jax.ShapeDtypeStruct((height, strips * wide), jnp.bfloat16),
        in_specs=[
            pl.BlockSpec(memory_space=pltpu.SMEM),
            pl.BlockSpec(memory_space=pltpu.VMEM),
        ],
        out_specs=pl.BlockSpec(memory_space=pl.ANY),
        scratch_shapes=[
            pltpu.VMEM((strips, height, wide), jnp.bfloat16),
            pltpu.SemaphoreType.DMA((strips,)),
        ],
        cost_estimate=cost(0, 4 * height * strips * wide),
        compiler_params=params(16 * 1024 * 1024),
    )(ys, received)


def per_device(tokens, dec_bias, enc_weight, enc_bias):
    own, width = tokens.shape
    rows, slab = enc_weight.shape
    lane = slab // (2 * CHIPS * CORES * XLO)
    total = own * CHIPS * CORES
    core = lax.axis_index("c")
    xlo = lax.axis_index("xl")
    y = lax.axis_index("y")
    chip = y * 2 + lax.axis_index("xh")
    z = lax.axis_index("z")
    which = jnp.reshape(core, (1,)).astype(jnp.int32)
    ys = lax.rem(jnp.stack([y, y + 3, y + 1, y + 2]), YS).astype(jnp.int32)

    centered = (tokens.astype(jnp.float32) - dec_bias).astype(jnp.bfloat16)
    halves = centered.reshape(own, CHIPS, CORES, rows).transpose(2, 0, 1, 3)
    halves = halves.reshape(CORES, own, CHIPS * rows)
    keep = jnp.where(core == 0, halves[0], halves[1])
    give = jnp.where(core == 0, halves[1], halves[0])
    got = lax.ppermute(give, "c", SWAP)
    mine = jnp.where(core == xlo, keep, got)
    part = own // DEPTH
    mine = lax.dynamic_slice_in_dim(mine, z * part, part, 0)
    near = spread(mine, PLANE, PEERS).reshape(total // DEPTH, CHIPS * rows)
    pieces = [near]
    low = high = near
    for _ in range(DEPTH // 2 - 1):
        low = lax.ppermute(low, "z", shift("z", 1))
        high = lax.ppermute(high, "z", shift("z", -1))
        pieces += [low, high]
    cut = near.shape[0] // 2
    pieces.append(lax.ppermute(low[:cut], "z", shift("z", 1)))
    pieces.append(lax.ppermute(high[cut:], "z", shift("z", -1)))
    batch = collect(jnp.reshape(z, (1,)).astype(jnp.int32), pieces)

    biases = enc_bias.reshape(2, CHIPS, CORES, XLO, lane)
    biases = lax.dynamic_index_in_dim(biases, chip, 1, keepdims=False)
    biases = lax.dynamic_index_in_dim(biases, core, 1, keepdims=False)
    bias_keep = lax.dynamic_index_in_dim(biases, xlo, 1, keepdims=False)
    bias_give = lax.dynamic_index_in_dim(biases, 1 - xlo, 1, keepdims=False)
    bias_got = lax.ppermute(bias_give, "xl", SWAP)
    bias = jnp.where(xlo == 0, jnp.stack([bias_keep, bias_got]), jnp.stack([bias_got, bias_keep]))

    weight = exchange(regroup(enc_weight, lane), PLANE)
    sums, sent = encode(which, batch, weight, lane)
    other = lax.ppermute(sent, "c", SWAP)
    low, high, *turned = finish(sums, other, bias)
    held = jnp.concatenate(turned, axis=1)

    def reach(held, step, sources):
        up = lax.ppermute(held, "z", [(i, (i + step) % DEPTH) for i in sources[0]])
        down = lax.ppermute(held, "z", [(i, (i - step) % DEPTH) for i in sources[1]])
        for moved, origins, sign in ((up, sources[0], 1), (down, sources[1], -1)):
            for i in origins:
                held = jnp.where(z == (i + sign * step) % DEPTH, moved, held)
        return held

    size = MATES // CORES
    forth = [(i, (i + 1) % size) for i in range(size)]
    back = [(i, (i - 1) % size) for i in range(size)]
    held = reach(held, 3, ((0,), (0,)))
    below_high = lax.ppermute(high, "y", shift("y", 1))
    above_low = lax.ppermute(low, "y", shift("y", -1))
    held, below_high, above_low = lax.optimization_barrier((held, below_high, above_low))
    held = reach(held, 1, ((0, 3, 5), (0, 3)))
    below_low = lax.ppermute(low, "y", shift("y", 1))
    above_high = lax.ppermute(high, "y", shift("y", -1))
    held, below_low, above_high = lax.optimization_barrier((held, below_low, above_high))
    left = lax.ppermute(held, LINE, forth)
    right = lax.ppermute(held, LINE, back)
    far_low = lax.ppermute(above_low, "y", shift("y", -1))
    far_high = lax.ppermute(below_high, "y", shift("y", 1))
    over = lax.ppermute(held, LINE, [(i, (i + 2) % size) for i in range(size)])
    over, far_low, far_high = lax.optimization_barrier((over, far_low, far_high))
    here = jnp.reshape(lax.axis_index("xh") * XLO + xlo, (1,)).astype(jnp.int32)
    panel = assemble(here, (held, left, right, over), size)
    theirs = lax.ppermute(panel, "c", SWAP)

    acts = (low, high, below_low, below_high, above_low, above_high, far_low, far_high)
    sent, ys = lax.optimization_barrier((gram(which, panel, theirs, acts), ys))
    return place(ys, exchange(sent, ROW))


def solution(mesh):
    fine = Mesh(mesh.devices.reshape(SIZES), AXES)
    return jax.shard_map(
        per_device,
        mesh=fine,
        in_specs=(P(TOK, None), P(), P(TOK, LATENT), P(LATENT)),
        out_specs=P(TOK, LATENT),
        check_vma=False,
    )
```
